32 devices in a mesh: groups: 2 (over x), dp: 16 (over z, y, core).
Axes of the slice: x: 2, y: 2, z: 4, core: 2. Of those that a mesh axis runs over, the one named last changes fastest.
Arguments:
- layer_inputs: bfloat16 [128, 64, 4096], P(('groups', 'dp')), parts along dimension 0, may hold values from -6 to 6
- out_grads: bfloat16 [128, 64, 14336], P(('groups', 'dp')), parts along dimension 0, may hold values from -6 to 6
- lengths: int32 [128], P(('groups', 'dp')), parts along dimension 0, may hold values from 1 to 64
- p_in: bfloat16 [32, 4096], replicated, may hold values from -0.09375 to 0.09375
- p_out: bfloat16 [64, 14336], replicated, may hold values from -0.046875 to 0.046875
- test_proj: bfloat16 [128, 2048], P(('groups', 'dp')), parts along dimension 0, may hold values from -6 to 6
Outputs:
- fisher: float32 [4096, 2048], P(('groups', 'dp')), parts along dimension 0
- scores: float32 [128, 64], P(('groups', 'dp')), parts along dimension 0
The draws below stay inside these ranges and needn't reach their ends.
There are 2 independent parts, one for each index of `groups`. The reference program is written for one: setup_inputs(seed, part) draws one part's arguments, and reference() takes and returns one part's arrays. A program takes and returns all parts, laid end to end along the dimension named above; an argument that names none is the same for every part. Nothing has to cross between parts.
All inputs are finite; a program needn't handle non-finite values.
Results may differ from the reference program's by a relative error of at most 0.015.
Values may be sent and summed in bfloat16 or wider, within the bound.
A program may use at most 128 MiB of HBM per device.

```python
import jax
import jax.numpy as jnp
from jax import lax

D = 4096
FF = 14336
K_IN = 32
K_OUT = 64
LEN = 64
F = 2048
SEQS = 64
TEST = 64


def touch_ends(values, key, low, largest):
    place = [jax.random.randint(jax.random.fold_in(key, axis), (), 0, length) for axis, length in enumerate(values.shape)]
    longest = values.shape.index(max(values.shape))
    next_to = place[:longest] + [(place[longest] + 1) % values.shape[longest]] + place[longest + 1:]
    return values.at[tuple(place)].set(low).at[tuple(next_to)].set(largest)


def shard_levels(key, extent, cuts, smallest, largest):
    level, own = 1.0, jax.random.fold_in(key, 6)
    for position, blocks in cuts:
        steps = jnp.exp(jax.random.uniform(jax.random.fold_in(own, position), (blocks,), jnp.float32, smallest / len(cuts), largest / len(cuts)))
        level = level * jnp.repeat(steps, extent[position] // blocks).reshape([-1 if axis == position else 1 for axis in range(len(extent))])
    return level


def centred(own_key, extent, scale, most, cuts=(), held_as=jnp.bfloat16):
    loudness = shard_levels(own_key, extent, cuts, -0.22, 0.18) if cuts else 1.0
    entries = jax.random.normal(own_key, extent, jnp.float32) * scale * loudness
    return jnp.minimum(jnp.maximum(entries, -most), most).astype(held_as)


def setup_inputs(seed: int = 0, part: int = 0) -> dict:
    seeds = jax.random.split(jax.random.key(seed), 7)
    part_splits = jax.random.split(jax.random.fold_in(seeds[6], part), 7)
    return {
        "layer_inputs": centred(part_splits[0], (SEQS, LEN, D), 1.0, 6.0, ((0, 16),)),
        "out_grads": centred(part_splits[1], (SEQS, LEN, FF), 1.0, 6.0, ((0, 16),)),
        "lengths": touch_ends(jax.random.randint(part_splits[2], (SEQS,), 1, LEN + 1), jax.random.fold_in(part_splits[2], 1), 1, LEN).astype(jnp.int32),
        "p_in": centred(seeds[3], (K_IN, D), D ** -0.5, 0.09375),
        "p_out": centred(seeds[4], (K_OUT, FF), FF ** -0.5, 0.046875),
        "test_proj": centred(part_splits[5], (TEST, F), 1.0, 6.0, ((0, 16),)),
    }


def reference(layer_inputs, out_grads, lengths, p_in, p_out, test_proj):
    seq_count = layer_inputs.shape[0]
    live = (jnp.arange(LEN)[None, :] < lengths[:, None]).astype(jnp.float32)
    left = jnp.dot(layer_inputs.reshape(seq_count * LEN, D), p_in.T, preferred_element_type=jnp.float32).reshape(seq_count, LEN, K_IN)
    right = jnp.dot(out_grads.reshape(seq_count * LEN, FF), p_out.T, preferred_element_type=jnp.float32).reshape(seq_count, LEN, K_OUT)
    right = right * live[:, :, None]
    proj = jnp.einsum('slo,sli->soi', right, left).reshape(seq_count, F).astype(jnp.bfloat16)
    gram = jnp.dot(proj.T, proj, preferred_element_type=jnp.float32)
    proj_wide = proj.astype(jnp.float32)
    trace = jnp.sum(proj_wide * proj_wide)
    fisher = gram * (F / trace)
    test_wide = test_proj.astype(jnp.float32)
    rms_train = jnp.sqrt(lax.optimization_barrier(jnp.mean(proj_wide * proj_wide, axis=1)) + 1e-06)
    rms_test = jnp.sqrt(lax.optimization_barrier(jnp.mean(test_wide * test_wide, axis=1)) + 1e-06)
    inner = jnp.dot(proj, test_proj.T, preferred_element_type=jnp.float32)
    scores = inner / (rms_train[:, None] * rms_test[None, :] * jnp.sqrt(jnp.float32(F)))
    return (fisher, scores)
```

```python
import jax
import jax.numpy as jnp
from jax import lax
from jax.sharding import PartitionSpec as P


def local(layer_inputs, out_grads, lengths, p_in, p_out, test_proj):
    seq_count, seq_len, model_width = layer_inputs.shape
    hidden_width = out_grads.shape[2]
    test_all = lax.all_gather(test_proj, "dp", axis=0, tiled=True)
    live_mask = (jnp.arange(seq_len)[None, :] < lengths[:, None]).astype(jnp.float32)
    left_proj = jnp.dot(
        layer_inputs.reshape(seq_count * seq_len, model_width),
        p_in.T,
        preferred_element_type=jnp.float32,
    ).reshape(seq_count, seq_len, p_in.shape[0])
    right_proj = jnp.dot(
        out_grads.reshape(seq_count * seq_len, hidden_width),
        p_out.T,
        preferred_element_type=jnp.float32,
    ).reshape(seq_count, seq_len, p_out.shape[0])
    right_proj = right_proj * live_mask[:, :, None]
    features = p_in.shape[0] * p_out.shape[0]
    proj = (
        jnp.einsum("slo,sli->soi", right_proj, left_proj)
        .reshape(seq_count, features)
        .astype(jnp.bfloat16)
    )
    row_count = features // lax.axis_size("dp")
    first_row = lax.axis_index("dp") * row_count
    proj_all = lax.all_gather(proj, "dp", axis=0, tiled=True)
    mine = lax.dynamic_slice_in_dim(proj_all, first_row, row_count, 1)
    gram_rows = jnp.dot(mine.T, proj_all, preferred_element_type=jnp.float32)
    all_wide = proj_all.astype(jnp.float32)
    trace = jnp.sum(all_wide * all_wide)
    fisher = gram_rows * (features / trace)
    proj_wide = proj.astype(jnp.float32)
    rms_train = jnp.sqrt(jnp.mean(proj_wide * proj_wide, axis=1) + 1e-06)
    root_features = jnp.sqrt(jnp.float32(features))
    test_wide = test_all.astype(jnp.float32)
    rms_test = jnp.sqrt(jnp.mean(test_wide * test_wide, axis=1) + 1e-06)
    inner = jnp.dot(proj, test_all.T, preferred_element_type=jnp.float32)
    scores = inner / (rms_train[:, None] * rms_test[None, :] * root_features)
    return (fisher, scores)


def solution(mesh):
    return jax.shard_map(
        local,
        mesh=mesh,
        in_specs=(
            P(("groups", "dp"), None, None),
            P(("groups", "dp"), None, None),
            P(("groups", "dp")),
            P(),
            P(),
            P(("groups", "dp"), None),
        ),
        out_specs=(P(("groups", "dp"), None), P(("groups", "dp"), None)),
        check_vma=False,
    )
```

```python
import functools

import jax
import jax.numpy as jnp
from jax import lax
from jax.experimental import pallas as pl
from jax.experimental.pallas import tpu as pltpu
from jax.sharding import PartitionSpec as P

LANES = 128
HALVES = 2
MESH = pl.DeviceIdType.MESH


def chunk_count(width):
    for count in (7, 4, 2, 1):
        if width % (count * LANES) == 0:
            return count
    return 1


def dot_last(a, b):
    return lax.dot_general(a, b, (((1,), (1,)), ((), ())), preferred_element_type=jnp.float32)


def dot_first(a, b):
    return lax.dot_general(a, b, (((0,), (0,)), ((), ())), preferred_element_type=jnp.float32)


def hi_lo(a):
    hi = a.astype(jnp.bfloat16)
    return hi, (a - hi.astype(jnp.float32)).astype(jnp.bfloat16)


def kernel(
    n, k_in, k_out,
    len_ref, x_hbm, g_hbm, pin_hbm, pout_hbm, test_ref,
    fisher_ref, scores_ref,
    x_v, g_v, pin_v, pout_v,
    gath0, gath1, gtest,
    wide, wide_test, blocks, test_rows, fold, own, own_test, gram_tmp,
    sem_x, sem_g, sem_pin, sem_pout,
    send_a, send_b, recv,
):
    seqs, seq_len, _ = x_hbm.shape
    per = seqs // HALVES
    group_rows = LANES // k_in
    features = k_in * k_out
    nb = features // LANES
    chips = n // 2
    chunks = g_v.shape[1]
    width = g_v.shape[4]
    all_seqs = n * seqs

    me = lax.axis_index("dp")
    groups_me = lax.axis_index("groups")
    core = lax.rem(me, 2)
    chip = me // 2
    mate = chip * 2 + 1 - core

    def peer(k):
        return lax.rem(chip + k, chips) * 2 + core

    def x_copy(h):
        return pltpu.make_async_copy(x_hbm.at[pl.ds(h * per, per)], x_v.at[h], sem_x.at[h])

    def g_copy(h, c):
        start = pl.multiple_of(c * width, LANES)
        return pltpu.make_async_copy(
            g_hbm.at[pl.ds(h * per, per), :, pl.ds(start, width)], g_v.at[h, c], sem_g.at[h, c]
        )

    def pout_copy(c):
        start = pl.multiple_of(c * width, LANES)
        return pltpu.make_async_copy(pout_hbm.at[:, pl.ds(start, width)], pout_v.at[c], sem_pout.at[c])

    pin_copy = pltpu.make_async_copy(pin_hbm, pin_v, sem_pin)

    pin_copy.start()
    x_copy(0).start()

    @pl.loop(0, chunks)
    def _(c):
        pout_copy(c).start()
        g_copy(0, c).start()

    x_copy(1).start()

    @pl.loop(0, chunks)
    def _(c):
        g_copy(1, c).start()

    barrier = pltpu.get_barrier_semaphore()
    pl.semaphore_signal(barrier, inc=1, device_id=(groups_me, mate), device_id_type=MESH)

    @pl.loop(1, chips)
    def _(k):
        pl.semaphore_signal(barrier, inc=1, device_id=(groups_me, peer(k)), device_id_type=MESH)

    test_wide = test_ref[...].astype(jnp.float32)
    for b in range(nb):
        own_test[pl.ds(b, seqs, stride=nb), :] = test_wide[:, b * LANES:(b + 1) * LANES]
    gtest[me] = own_test[...].astype(jnp.bfloat16)

    pl.semaphore_wait(barrier, chips)

    def own_send(kind, buf, k):
        return pltpu.make_async_remote_copy(
            src_ref=buf.at[me], dst_ref=buf.at[me],
            send_sem=send_a.at[kind, k], recv_sem=recv.at[kind, me],
            device_id=(groups_me, peer(k)), device_id_type=MESH,
        )

    def forward(kind, buf, src, k):
        return pltpu.make_async_remote_copy(
            src_ref=buf.at[src], dst_ref=buf.at[src],
            send_sem=send_b.at[kind, k], recv_sem=recv.at[kind, src],
            device_id=(groups_me, mate), device_id_type=MESH,
        )

    def arrived(kind, buf, src):
        return pltpu.make_async_remote_copy(
            src_ref=buf.at[src], dst_ref=buf.at[src],
            send_sem=send_b.at[kind, 0], recv_sem=recv.at[kind, src],
            device_id=(groups_me, mate), device_id_type=MESH,
        )

    def send_own(kind, buf):
        @pl.loop(1, chips)
        def _(k):
            own_send(kind, buf, k).start()

        forward(kind, buf, me, 0).start()

    def pass_on(kind, buf):
        @pl.loop(1, chips)
        def _(k):
            src = peer(k)
            arrived(kind, buf, src).wait_recv()
            forward(kind, buf, src, k).start()

    def rest(kind, buf):
        @pl.loop(0, chips)
        def _(k):
            src = lax.rem(chip + k, chips) * 2 + 1 - core
            arrived(kind, buf, src).wait_recv()

    def drain(kind, buf):
        forward(kind, buf, me, 0).wait_send()

        @pl.loop(1, chips)
        def _(k):
            own_send(kind, buf, k).wait_send()
            forward(kind, buf, peer(k), k).wait_send()

    send_own(0, gtest)

    lane = lax.broadcasted_iota(jnp.int32, (nb, LANES), 1) // k_in
    token = lax.broadcasted_iota(jnp.int32, (seq_len, k_out), 0)

    pin_copy.wait()

    def right_part(h, low, high, total, first):
        def step(c, total):
            if first:
                pout_copy(c).wait()
            g_copy(h, c).wait()
            return total + dot_last(g_v[h, c].reshape(per * seq_len, width), pout_v[c])
        return lax.fori_loop(low, high, step, total)

    def finish(h, left, right, buf):
        for q in range(per):
            s = h * per + q
            rows = slice(q * seq_len, (q + 1) * seq_len)
            live = jnp.where(token < len_ref[s], right[rows], 0.0)
            rh, rl = hi_lo(live)
            lh, ll = hi_lo(left[rows])
            prod = dot_first(
                jnp.concatenate([rh, rh, rl], axis=0), jnp.concatenate([lh, ll, lh], axis=0)
            )
            fold[q] = prod
            tile = fold[q, pl.ds(0, nb, stride=group_rows), :]
            for k in range(1, group_rows):
                tile = jnp.where(lane == k, fold[q, pl.ds(k, nb, stride=group_rows), :], tile)
            tile = tile.astype(jnp.bfloat16)
            buf[me, q * nb:(q + 1) * nb, :] = tile
            own[s * nb:(s + 1) * nb, :] = tile.astype(jnp.float32)

    def left_part(h):
        x_copy(h).wait()
        pin = jnp.concatenate([pin_v[...]] * group_rows, axis=0)
        return dot_last(x_v[h].reshape(per * seq_len, x_v.shape[3]), pin)

    zero = jnp.zeros((per * seq_len, k_out), jnp.float32)
    mid = (chunks + 1) // 2

    left = left_part(0)
    right = right_part(0, 0, chunks, zero, True)
    finish(0, left, right, gath0)
    send_own(1, gath0)
    pass_on(0, gtest)

    left = left_part(1)
    right = right_part(1, 0, mid, zero, False)
    pass_on(1, gath0)
    right = right_part(1, mid, chunks, right, False)
    finish(1, left, right, gath1)
    send_own(2, gath1)

    rest(0, gtest)
    wide_test[...] = gtest[...].reshape(wide_test.shape).astype(jnp.float32)
    squares = jnp.zeros((all_seqs, LANES), jnp.float32)
    for b in range(nb):
        rows = wide_test[pl.ds(b, all_seqs, stride=nb), :]
        squares += rows * rows
        test_rows[:, b * LANES:(b + 1) * LANES] = rows.astype(jnp.bfloat16)
    own_rows = [own[pl.ds(b, seqs, stride=nb), :] for b in range(nb)]
    own_squares = own_rows[0] * own_rows[0]
    for b in range(1, nb):
        own_squares += own_rows[b] * own_rows[b]
    mean_train = jnp.sum(own_squares, axis=1, keepdims=True) / features
    mean_test = lax.dot_general(
        jnp.ones((seqs, LANES), jnp.float32), squares, (((1,), (1,)), ((), ())),
        precision=lax.Precision.HIGHEST, preferred_element_type=jnp.float32,
    ) / features
    inner = dot_last(jnp.concatenate(own_rows, axis=1).astype(jnp.bfloat16), test_rows[...])
    scores_ref[...] = inner / (
        jnp.sqrt(mean_train + 1e-06) * jnp.sqrt(mean_test + 1e-06) * jnp.sqrt(jnp.float32(features))
    )

    rest(1, gath0)
    half_rows = n * per * nb
    half_seqs = n * per

    def spread(h, buf):
        wide[pl.ds(h * half_rows, half_rows), :] = buf[...].reshape(half_rows, LANES).astype(jnp.float32)
        total = jnp.zeros((half_seqs, LANES), jnp.float32)
        for b in range(nb):
            rows = wide[pl.ds(h * half_rows + b, half_seqs, stride=nb), :]
            total += rows * rows
            blocks[b, h * half_seqs:(h + 1) * half_seqs, :] = rows.astype(jnp.bfloat16)
        return total

    total = spread(0, gath0)
    pass_on(2, gath1)
    rest(2, gath1)
    total += spread(1, gath1)
    scale = features / jnp.sum(total)

    row_count = fisher_ref.shape[0]
    first_row = me * row_count
    if row_count % LANES == 0:
        for r in range(row_count // LANES):
            mine = blocks[first_row // LANES + r]
            for b in range(nb):
                fisher_ref[r * LANES:(r + 1) * LANES, b * LANES:(b + 1) * LANES] = (
                    dot_first(mine, blocks[b]) * scale
                )
    else:
        mine = blocks[first_row // LANES]
        offset = pl.multiple_of(lax.rem(first_row, LANES), row_count)
        for b in range(nb):
            gram_tmp[...] = dot_first(mine, blocks[b]) * scale
            fisher_ref[:, b * LANES:(b + 1) * LANES] = gram_tmp[pl.ds(offset, row_count), :]

    drain(0, gtest)
    drain(1, gath0)
    drain(2, gath1)


def local(layer_inputs, out_grads, lengths, p_in, p_out, test_proj):
    n = lax.axis_size("dp")
    seqs, seq_len, model_width = layer_inputs.shape
    hidden = out_grads.shape[2]
    k_in, k_out = p_in.shape[0], p_out.shape[0]
    features = k_in * k_out
    nb = features // LANES
    chunks = chunk_count(hidden)
    width = hidden // chunks
    per = seqs // HALVES
    chips = n // 2
    f32, bf16 = jnp.float32, jnp.bfloat16
    dma = pltpu.SemaphoreType.DMA
    anywhere = pl.BlockSpec(memory_space=pl.ANY)
    vmem = pl.BlockSpec(memory_space=pltpu.VMEM)
    return pl.pallas_call(
        functools.partial(kernel, n, k_in, k_out),
        out_shape=(
            jax.ShapeDtypeStruct((features // n, features), f32),
            jax.ShapeDtypeStruct((seqs, n * seqs), f32),
        ),
        in_specs=[pl.BlockSpec(memory_space=pltpu.SMEM)] + [anywhere] * 4 + [vmem],
        out_specs=(vmem, vmem),
        scratch_shapes=[
            pltpu.VMEM((HALVES, per, seq_len, model_width), bf16),
            pltpu.VMEM((HALVES, chunks, per, seq_len, width), bf16),
            pltpu.VMEM((k_in, model_width), bf16),
            pltpu.VMEM((chunks, k_out, width), bf16),
            pltpu.VMEM((n, per * nb, LANES), bf16),
            pltpu.VMEM((n, per * nb, LANES), bf16),
            pltpu.VMEM((n, seqs * nb, LANES), bf16),
            pltpu.VMEM((n * seqs * nb, LANES), f32),
            pltpu.VMEM((n * seqs * nb, LANES), f32),
            pltpu.VMEM((nb, n * seqs, LANES), bf16),
            pltpu.VMEM((n * seqs, features), bf16),
            pltpu.VMEM((per, k_out, LANES), f32),
            pltpu.VMEM((seqs * nb, LANES), f32),
            pltpu.VMEM((seqs * nb, LANES), f32),
            pltpu.VMEM((LANES, LANES), f32),
            dma((HALVES,)),
            dma((HALVES, chunks)),
            dma,
            dma((chunks,)),
            dma((3, chips)),
            dma((3, chips)),
            dma((3, n)),
        ],
        compiler_params=pltpu.CompilerParams(
            collective_id=0, has_side_effects=True, vmem_limit_bytes=48 * 1024 * 1024
        ),
        cost_estimate=pl.CostEstimate(
            flops=2 * seqs * seq_len * (hidden * k_out + model_width * k_in),
            bytes_accessed=2 * (seqs * seq_len + k_out) * hidden,
            transcendentals=0,
        ),
    )(lengths, layer_inputs, out_grads, p_in, p_out, test_proj)


def solution(mesh):
    return jax.shard_map(
        local,
        mesh=mesh,
        in_specs=(
            P(("groups", "dp"), None, None),
            P(("groups", "dp"), None, None),
            P(("groups", "dp")),
            P(),
            P(),
            P(("groups", "dp"), None),
        ),
        out_specs=(P(("groups", "dp"), None), P(("groups", "dp"), None)),
        check_vma=False,
    )
```

```python
import functools

import jax
import jax.numpy as jnp
from jax import lax
from jax.experimental import pallas as pl
from jax.experimental.pallas import tpu as pltpu
from jax.sharding import PartitionSpec as P

LANES = 128
HALVES = 2
MESH = pl.DeviceIdType.MESH


def chunk_count(width):
    for count in (7, 4, 2, 1):
        if width % (count * LANES) == 0:
            return count
    return 1


def dot_last(a, b):
    return lax.dot_general(a, b, (((1,), (1,)), ((), ())), preferred_element_type=jnp.float32)


def dot_first(a, b):
    return lax.dot_general(a, b, (((0,), (0,)), ((), ())), preferred_element_type=jnp.float32)


def hi_lo(a):
    hi = a.astype(jnp.bfloat16)
    return hi, (a - hi.astype(jnp.float32)).astype(jnp.bfloat16)


def kernel(
    n, k_in, k_out,
    len_ref, x_hbm, g_hbm, pin_hbm, pout_hbm, test_hbm,
    fisher_ref, scores_ref,
    x_v, g_v, pin_v, pout_v, test_v,
    gath0, gath1, gtest,
    wide, wide_test, blocks, test_rows, fold, own, own_test, gram_tmp,
    sem_x, sem_g, sem_pin, sem_pout, sem_test,
    send, recv,
):
    seqs, seq_len, _ = x_hbm.shape
    per = seqs // HALVES
    group_rows = LANES // k_in
    features = k_in * k_out
    nb = features // LANES
    chunks = g_v.shape[1]
    width = g_v.shape[4]
    all_seqs = n * seqs

    me = lax.axis_index("dp")
    groups_me = lax.axis_index("groups")
    def peer(k):
        return lax.rem(me + k, n)

    def x_copy(h):
        return pltpu.make_async_copy(x_hbm.at[pl.ds(h * per, per)], x_v.at[h], sem_x.at[h])

    def g_copy(h, c):
        start = pl.multiple_of(c * width, LANES)
        return pltpu.make_async_copy(
            g_hbm.at[pl.ds(h * per, per), :, pl.ds(start, width)], g_v.at[h, c], sem_g.at[h, c]
        )

    def pout_copy(c):
        start = pl.multiple_of(c * width, LANES)
        return pltpu.make_async_copy(pout_hbm.at[:, pl.ds(start, width)], pout_v.at[c], sem_pout.at[c])

    pin_copy = pltpu.make_async_copy(pin_hbm, pin_v, sem_pin)

    test_copy = pltpu.make_async_copy(test_hbm, test_v, sem_test)

    test_copy.start()
    pin_copy.start()
    x_copy(0).start()

    @pl.loop(0, chunks)
    def _(c):
        pout_copy(c).start()
        g_copy(0, c).start()

    x_copy(1).start()

    @pl.loop(0, chunks)
    def _(c):
        g_copy(1, c).start()

    barrier = pltpu.get_barrier_semaphore()

    @pl.loop(1, n)
    def _(k):
        pl.semaphore_signal(barrier, inc=1, device_id=(groups_me, peer(k)), device_id_type=MESH)

    test_copy.wait()
    test_wide = test_v[...].astype(jnp.float32)
    for b in range(nb):
        own_test[pl.ds(b, seqs, stride=nb), :] = test_wide[:, b * LANES:(b + 1) * LANES]
    gtest[me] = own_test[...].astype(jnp.bfloat16)

    pl.semaphore_wait(barrier, n - 1)

    def push(kind, buf, k):
        return pltpu.make_async_remote_copy(
            src_ref=buf.at[me], dst_ref=buf.at[me],
            send_sem=send.at[kind, k], recv_sem=recv.at[kind, me],
            device_id=(groups_me, peer(k)), device_id_type=MESH,
        )

    def pull(kind, buf, k):
        src = peer(k)
        return pltpu.make_async_remote_copy(
            src_ref=buf.at[src], dst_ref=buf.at[src],
            send_sem=send.at[kind, k], recv_sem=recv.at[kind, src],
            device_id=(groups_me, src), device_id_type=MESH,
        )

    def send_own(kind, buf):
        @pl.loop(1, n)
        def _(k):
            push(kind, buf, k).start()

    def rest(kind, buf):
        @pl.loop(1, n)
        def _(k):
            pull(kind, buf, k).wait_recv()

    def drain(kind, buf):
        @pl.loop(1, n)
        def _(k):
            push(kind, buf, k).wait_send()

    send_own(0, gtest)

    lane = lax.broadcasted_iota(jnp.int32, (nb, LANES), 1) // k_in
    token = lax.broadcasted_iota(jnp.int32, (seq_len, k_out), 0)

    pin_copy.wait()

    def right_part(h, low, high, total, first):
        def step(c, total):
            if first:
                pout_copy(c).wait()
            g_copy(h, c).wait()
            return total + dot_last(g_v[h, c].reshape(per * seq_len, width), pout_v[c])
        return lax.fori_loop(low, high, step, total)

    def finish(h, left, right, buf):
        for q in range(per):
            s = h * per + q
            rows = slice(q * seq_len, (q + 1) * seq_len)
            live = jnp.where(token < len_ref[s], right[rows], 0.0)
            rh, rl = hi_lo(live)
            lh, ll = hi_lo(left[rows])
            prod = dot_first(
                jnp.concatenate([rh, rh, rl], axis=0), jnp.concatenate([lh, ll, lh], axis=0)
            )
            fold[q] = prod
            tile = fold[q, pl.ds(0, nb, stride=group_rows), :]
            for k in range(1, group_rows):
                tile = jnp.where(lane == k, fold[q, pl.ds(k, nb, stride=group_rows), :], tile)
            tile = tile.astype(jnp.bfloat16)
            buf[me, q * nb:(q + 1) * nb, :] = tile
            own[s * nb:(s + 1) * nb, :] = tile.astype(jnp.float32)

    def left_part(h):
        x_copy(h).wait()
        pin = jnp.concatenate([pin_v[...]] * group_rows, axis=0)
        return dot_last(x_v[h].reshape(per * seq_len, x_v.shape[3]), pin)

    zero = jnp.zeros((per * seq_len, k_out), jnp.float32)
    mid = (chunks + 1) // 2

    left = left_part(0)
    right = right_part(0, 0, chunks, zero, True)
    finish(0, left, right, gath0)
    send_own(1, gath0)

    left = left_part(1)
    right = right_part(1, 0, mid, zero, False)
    right = right_part(1, mid, chunks, right, False)
    finish(1, left, right, gath1)
    send_own(2, gath1)

    rest(0, gtest)
    wide_test[...] = gtest[...].reshape(wide_test.shape).astype(jnp.float32)
    squares = jnp.zeros((all_seqs, LANES), jnp.float32)
    for b in range(nb):
        rows = wide_test[pl.ds(b, all_seqs, stride=nb), :]
        squares += rows * rows
        test_rows[:, b * LANES:(b + 1) * LANES] = rows.astype(jnp.bfloat16)
    own_rows = [own[pl.ds(b, seqs, stride=nb), :] for b in range(nb)]
    own_squares = own_rows[0] * own_rows[0]
    for b in range(1, nb):
        own_squares += own_rows[b] * own_rows[b]
    mean_train = jnp.sum(own_squares, axis=1, keepdims=True) / features
    mean_test = lax.dot_general(
        jnp.ones((seqs, LANES), jnp.float32), squares, (((1,), (1,)), ((), ())),
        precision=lax.Precision.HIGHEST, preferred_element_type=jnp.float32,
    ) / features
    inner = dot_last(jnp.concatenate(own_rows, axis=1).astype(jnp.bfloat16), test_rows[...])
    scores_ref[...] = inner / (
        jnp.sqrt(mean_train + 1e-06) * jnp.sqrt(mean_test + 1e-06) * jnp.sqrt(jnp.float32(features))
    )

    rest(1, gath0)
    half_rows = n * per * nb
    half_seqs = n * per

    def spread(h, buf):
        wide[pl.ds(h * half_rows, half_rows), :] = buf[...].reshape(half_rows, LANES).astype(jnp.float32)
        total = jnp.zeros((half_seqs, LANES), jnp.float32)
        for b in range(nb):
            rows = wide[pl.ds(h * half_rows + b, half_seqs, stride=nb), :]
            total += rows * rows
            blocks[b, h * half_seqs:(h + 1) * half_seqs, :] = rows.astype(jnp.bfloat16)
        return total

    total = spread(0, gath0)
    rest(2, gath1)
    total += spread(1, gath1)
    scale = features / jnp.sum(total)

    row_count = fisher_ref.shape[0]
    first_row = me * row_count
    if row_count % LANES == 0:
        for r in range(row_count // LANES):
            mine = blocks[first_row // LANES + r]
            for b in range(nb):
                fisher_ref[r * LANES:(r + 1) * LANES, b * LANES:(b + 1) * LANES] = (
                    dot_first(mine, blocks[b]) * scale
                )
    else:
        mine = blocks[first_row // LANES]
        offset = pl.multiple_of(lax.rem(first_row, LANES), row_count)
        for b in range(nb):
            gram_tmp[...] = dot_first(mine, blocks[b]) * scale
            fisher_ref[:, b * LANES:(b + 1) * LANES] = gram_tmp[pl.ds(offset, row_count), :]

    drain(0, gtest)
    drain(1, gath0)
    drain(2, gath1)


def local(layer_inputs, out_grads, lengths, p_in, p_out, test_proj):
    n = lax.axis_size("dp")
    seqs, seq_len, model_width = layer_inputs.shape
    hidden = out_grads.shape[2]
    k_in, k_out = p_in.shape[0], p_out.shape[0]
    features = k_in * k_out
    nb = features // LANES
    chunks = chunk_count(hidden)
    width = hidden // chunks
    per = seqs // HALVES
    f32, bf16 = jnp.float32, jnp.bfloat16
    dma = pltpu.SemaphoreType.DMA
    anywhere = pl.BlockSpec(memory_space=pltpu.HBM)
    vmem = pl.BlockSpec(memory_space=pltpu.VMEM)
    return pl.pallas_call(
        functools.partial(kernel, n, k_in, k_out),
        out_shape=(
            jax.ShapeDtypeStruct((features // n, features), f32),
            jax.ShapeDtypeStruct((seqs, n * seqs), f32),
        ),
        in_specs=[pl.BlockSpec(memory_space=pltpu.SMEM)] + [anywhere] * 5,
        out_specs=(vmem, vmem),
        scratch_shapes=[
            pltpu.VMEM((HALVES, per, seq_len, model_width), bf16),
            pltpu.VMEM((HALVES, chunks, per, seq_len, width), bf16),
            pltpu.VMEM((k_in, model_width), bf16),
            pltpu.VMEM((chunks, k_out, width), bf16),
            pltpu.VMEM((seqs, features), bf16),
            pltpu.VMEM((n, per * nb, LANES), bf16),
            pltpu.VMEM((n, per * nb, LANES), bf16),
            pltpu.VMEM((n, seqs * nb, LANES), bf16),
            pltpu.VMEM((n * seqs * nb, LANES), f32),
            pltpu.VMEM((n * seqs * nb, LANES), f32),
            pltpu.VMEM((nb, n * seqs, LANES), bf16),
            pltpu.VMEM((n * seqs, features), bf16),
            pltpu.VMEM((per, k_out, LANES), f32),
            pltpu.VMEM((seqs * nb, LANES), f32),
            pltpu.VMEM((seqs * nb, LANES), f32),
            pltpu.VMEM((LANES, LANES), f32),
            dma((HALVES,)),
            dma((HALVES, chunks)),
            dma,
            dma((chunks,)),
            dma,
            dma((3, n)),
            dma((3, n)),
        ],
        compiler_params=pltpu.CompilerParams(
            collective_id=0, has_side_effects=True, vmem_limit_bytes=57 * 1024 * 1024
        ),
        cost_estimate=pl.CostEstimate(
            flops=2 * seqs * seq_len * (hidden * k_out + model_width * k_in),
            bytes_accessed=2 * (seqs * seq_len + k_out) * hidden,
            transcendentals=0,
        ),
    )(lengths, layer_inputs, out_grads, p_in, p_out, test_proj)


def solution(mesh):
    return jax.shard_map(
        local,
        mesh=mesh,
        in_specs=(
            P(("groups", "dp"), None, None),
            P(("groups", "dp"), None, None),
            P(("groups", "dp")),
            P(),
            P(),
            P(("groups", "dp"), None),
        ),
        out_specs=(P(("groups", "dp"), None), P(("groups", "dp"), None)),
        check_vma=False,
    )
```

```python
import functools

import jax
import jax.numpy as jnp
from jax import lax
from jax.experimental import pallas as pl
from jax.experimental.pallas import tpu as pltpu
from jax.sharding import PartitionSpec as P

LANES = 128
HALVES = 2
MESH = pl.DeviceIdType.MESH


def chunk_count(width):
    for count in (7, 4, 2, 1):
        if width % (count * LANES) == 0:
            return count
    return 1


def dot_last(a, b):
    return lax.dot_general(a, b, (((1,), (1,)), ((), ())), preferred_element_type=jnp.float32)


def dot_first(a, b):
    return lax.dot_general(a, b, (((0,), (0,)), ((), ())), preferred_element_type=jnp.float32)


def hi_lo(a):
    hi = a.astype(jnp.bfloat16)
    return hi, (a - hi.astype(jnp.float32)).astype(jnp.bfloat16)


def kernel(
    n, k_in, k_out,
    len_ref, x_hbm, g_hbm, pin_hbm, pout_hbm, test_hbm,
    blocks, scale_ref, scores_ref,
    x_v, g_v, pin_v, pout_v, test_v,
    gath0, gath1, gtest,
    wide, wide_test, test_rows, fold, own, own_test,
    sem_x, sem_g, sem_pin, sem_pout, sem_test,
    send, recv,
):
    seqs, seq_len, _ = x_hbm.shape
    per = seqs // HALVES
    group_rows = LANES // k_in
    features = k_in * k_out
    nb = features // LANES
    chunks = g_v.shape[1]
    width = g_v.shape[4]
    all_seqs = n * seqs

    me = lax.axis_index("dp")
    groups_me = lax.axis_index("groups")
    def peer(k):
        return lax.rem(me + k, n)

    def x_copy(h):
        return pltpu.make_async_copy(x_hbm.at[pl.ds(h * per, per)], x_v.at[h], sem_x.at[h])

    def g_copy(h, c):
        start = pl.multiple_of(c * width, LANES)
        return pltpu.make_async_copy(
            g_hbm.at[pl.ds(h * per, per), :, pl.ds(start, width)], g_v.at[h, c], sem_g.at[h, c]
        )

    def pout_copy(c):
        start = pl.multiple_of(c * width, LANES)
        return pltpu.make_async_copy(pout_hbm.at[:, pl.ds(start, width)], pout_v.at[c], sem_pout.at[c])

    pin_copy = pltpu.make_async_copy(pin_hbm, pin_v, sem_pin)

    test_copy = pltpu.make_async_copy(test_hbm, test_v, sem_test)

    test_copy.start()
    pin_copy.start()
    x_copy(0).start()

    @pl.loop(0, chunks)
    def _(c):
        pout_copy(c).start()
        g_copy(0, c).start()

    x_copy(1).start()

    @pl.loop(0, chunks)
    def _(c):
        g_copy(1, c).start()

    barrier = pltpu.get_barrier_semaphore()

    @pl.loop(1, n)
    def _(k):
        pl.semaphore_signal(barrier, inc=1, device_id=(groups_me, peer(k)), device_id_type=MESH)

    test_copy.wait()
    test_wide = test_v[...].astype(jnp.float32)
    for b in range(nb):
        own_test[pl.ds(b, seqs, stride=nb), :] = test_wide[:, b * LANES:(b + 1) * LANES]
    gtest[me] = own_test[...].astype(jnp.bfloat16)

    pl.semaphore_wait(barrier, n - 1)

    def push(kind, buf, k):
        return pltpu.make_async_remote_copy(
            src_ref=buf.at[me], dst_ref=buf.at[me],
            send_sem=send.at[kind, k], recv_sem=recv.at[kind, me],
            device_id=(groups_me, peer(k)), device_id_type=MESH,
        )

    def pull(kind, buf, k):
        src = peer(k)
        return pltpu.make_async_remote_copy(
            src_ref=buf.at[src], dst_ref=buf.at[src],
            send_sem=send.at[kind, k], recv_sem=recv.at[kind, src],
            device_id=(groups_me, src), device_id_type=MESH,
        )

    def send_own(kind, buf):
        @pl.loop(1, n)
        def _(k):
            push(kind, buf, k).start()

    def rest(kind, buf):
        @pl.loop(1, n)
        def _(k):
            pull(kind, buf, k).wait_recv()

    def drain(kind, buf):
        @pl.loop(1, n)
        def _(k):
            push(kind, buf, k).wait_send()

    send_own(0, gtest)

    lane = lax.broadcasted_iota(jnp.int32, (nb, LANES), 1) // k_in
    token = lax.broadcasted_iota(jnp.int32, (seq_len, k_out), 0)

    pin_copy.wait()

    def right_part(h, low, high, total, first):
        def step(c, total):
            if first:
                pout_copy(c).wait()
            g_copy(h, c).wait()
            return total + dot_last(g_v[h, c].reshape(per * seq_len, width), pout_v[c])
        return lax.fori_loop(low, high, step, total)

    def finish(h, left, right, buf):
        for q in range(per):
            s = h * per + q
            rows = slice(q * seq_len, (q + 1) * seq_len)
            live = jnp.where(token < len_ref[s], right[rows], 0.0)
            rh, rl = hi_lo(live)
            lh, ll = hi_lo(left[rows])
            prod = dot_first(
                jnp.concatenate([rh, rh, rl], axis=0), jnp.concatenate([lh, ll, lh], axis=0)
            )
            fold[q] = prod
            tile = fold[q, pl.ds(0, nb, stride=group_rows), :]
            for k in range(1, group_rows):
                tile = jnp.where(lane == k, fold[q, pl.ds(k, nb, stride=group_rows), :], tile)
            tile = tile.astype(jnp.bfloat16)
            buf[me, q * nb:(q + 1) * nb, :] = tile
            own[s * nb:(s + 1) * nb, :] = tile.astype(jnp.float32)

    def left_part(h):
        x_copy(h).wait()
        pin = jnp.concatenate([pin_v[...]] * group_rows, axis=0)
        return dot_last(x_v[h].reshape(per * seq_len, x_v.shape[3]), pin)

    zero = jnp.zeros((per * seq_len, k_out), jnp.float32)
    mid = (chunks + 1) // 2

    left = left_part(0)
    right = right_part(0, 0, chunks, zero, True)
    finish(0, left, right, gath0)
    send_own(1, gath0)

    left = left_part(1)
    right = right_part(1, 0, mid, zero, False)
    right = right_part(1, mid, chunks, right, False)
    finish(1, left, right, gath1)
    send_own(2, gath1)

    rest(0, gtest)
    wide_test[...] = gtest[...].reshape(wide_test.shape).astype(jnp.float32)
    squares = jnp.zeros((all_seqs, LANES), jnp.float32)
    for b in range(nb):
        rows = wide_test[pl.ds(b, all_seqs, stride=nb), :]
        squares += rows * rows
        test_rows[:, b * LANES:(b + 1) * LANES] = rows.astype(jnp.bfloat16)
    own_rows = [own[pl.ds(b, seqs, stride=nb), :] for b in range(nb)]
    own_squares = own_rows[0] * own_rows[0]
    for b in range(1, nb):
        own_squares += own_rows[b] * own_rows[b]
    mean_train = jnp.sum(own_squares, axis=1, keepdims=True) / features
    mean_test = lax.dot_general(
        jnp.ones((seqs, LANES), jnp.float32), squares, (((1,), (1,)), ((), ())),
        precision=lax.Precision.HIGHEST, preferred_element_type=jnp.float32,
    ) / features
    inner = dot_last(jnp.concatenate(own_rows, axis=1).astype(jnp.bfloat16), test_rows[...])
    scores_ref[...] = inner / (
        jnp.sqrt(mean_train + 1e-06) * jnp.sqrt(mean_test + 1e-06) * jnp.sqrt(jnp.float32(features))
    )

    rest(1, gath0)
    half_rows = n * per * nb
    half_seqs = n * per

    def spread(h, buf):
        wide[pl.ds(h * half_rows, half_rows), :] = buf[...].reshape(half_rows, LANES).astype(jnp.float32)
        total = jnp.zeros((half_seqs, LANES), jnp.float32)
        for b in range(nb):
            rows = wide[pl.ds(h * half_rows + b, half_seqs, stride=nb), :]
            total += rows * rows
            blocks[b, h * half_seqs:(h + 1) * half_seqs, :] = rows.astype(jnp.bfloat16)
        return total

    total = spread(0, gath0)
    rest(2, gath1)
    total += spread(1, gath1)
    scale = features / jnp.sum(total)

    scale_ref[...] = jnp.full(scale_ref.shape, scale, jnp.float32)

    drain(0, gtest)
    drain(1, gath0)
    drain(2, gath1)


def gram_kernel(blocks, scale_ref, scores_in, fisher_ref, scores_ref, gram_tmp):
    me = lax.axis_index("dp")
    nb = blocks.shape[0]
    scale = scale_ref[0:1, :]
    scores_ref[...] = scores_in[...]
    row_count = fisher_ref.shape[0]
    first_row = me * row_count
    if row_count % LANES == 0:
        for r in range(row_count // LANES):
            mine = blocks[first_row // LANES + r]
            for b in range(nb):
                fisher_ref[r * LANES:(r + 1) * LANES, b * LANES:(b + 1) * LANES] = (
                    dot_first(mine, blocks[b]) * scale
                )
    else:
        mine = blocks[first_row // LANES]
        offset = pl.multiple_of(lax.rem(first_row, LANES), row_count)
        for b in range(nb):
            gram_tmp[...] = dot_first(mine, blocks[b]) * scale
            fisher_ref[:, b * LANES:(b + 1) * LANES] = gram_tmp[pl.ds(offset, row_count), :]


def local(layer_inputs, out_grads, lengths, p_in, p_out, test_proj):
    n = lax.axis_size("dp")
    seqs, seq_len, model_width = layer_inputs.shape
    hidden = out_grads.shape[2]
    k_in, k_out = p_in.shape[0], p_out.shape[0]
    features = k_in * k_out
    nb = features // LANES
    chunks = chunk_count(hidden)
    width = hidden // chunks
    per = seqs // HALVES
    f32, bf16 = jnp.float32, jnp.bfloat16
    dma = pltpu.SemaphoreType.DMA
    anywhere = pl.BlockSpec(memory_space=pltpu.HBM)
    vmem = pl.BlockSpec(memory_space=pltpu.VMEM)
    blocks, scale, scores = pl.pallas_call(
        functools.partial(kernel, n, k_in, k_out),
        out_shape=(
            jax.ShapeDtypeStruct((nb, n * seqs, LANES), bf16),
            jax.ShapeDtypeStruct((8, LANES), f32),
            jax.ShapeDtypeStruct((seqs, n * seqs), f32),
        ),
        in_specs=[pl.BlockSpec(memory_space=pltpu.SMEM)] + [anywhere] * 5,
        out_specs=(vmem, vmem, vmem),
        scratch_shapes=[
            pltpu.VMEM((HALVES, per, seq_len, model_width), bf16),
            pltpu.VMEM((HALVES, chunks, per, seq_len, width), bf16),
            pltpu.VMEM((k_in, model_width), bf16),
            pltpu.VMEM((chunks, k_out, width), bf16),
            pltpu.VMEM((seqs, features), bf16),
            pltpu.VMEM((n, per * nb, LANES), bf16),
            pltpu.VMEM((n, per * nb, LANES), bf16),
            pltpu.VMEM((n, seqs * nb, LANES), bf16),
            pltpu.VMEM((n * seqs * nb, LANES), f32),
            pltpu.VMEM((n * seqs * nb, LANES), f32),
            pltpu.VMEM((n * seqs, features), bf16),
            pltpu.VMEM((per, k_out, LANES), f32),
            pltpu.VMEM((seqs * nb, LANES), f32),
            pltpu.VMEM((seqs * nb, LANES), f32),
            dma((HALVES,)),
            dma((HALVES, chunks)),
            dma,
            dma((chunks,)),
            dma,
            dma((3, n)),
            dma((3, n)),
        ],
        compiler_params=pltpu.CompilerParams(
            collective_id=0, has_side_effects=True, vmem_limit_bytes=57 * 1024 * 1024
        ),
        cost_estimate=pl.CostEstimate(
            flops=2 * seqs * seq_len * (hidden * k_out + model_width * k_in),
            bytes_accessed=2 * (seqs * seq_len + k_out) * hidden,
            transcendentals=0,
        ),
    )(lengths, layer_inputs, out_grads, p_in, p_out, test_proj)
    return pl.pallas_call(
        gram_kernel,
        out_shape=(
            jax.ShapeDtypeStruct((features // n, features), f32),
            jax.ShapeDtypeStruct(scores.shape, f32),
        ),
        in_specs=[vmem, vmem, vmem],
        out_specs=(vmem, vmem),
        scratch_shapes=[pltpu.VMEM((LANES, LANES), f32)],
        compiler_params=pltpu.CompilerParams(vmem_limit_bytes=57 * 1024 * 1024),
    )(blocks, scale, scores)


def solution(mesh):
    return jax.shard_map(
        local,
        mesh=mesh,
        in_specs=(
            P(("groups", "dp"), None, None),
            P(("groups", "dp"), None, None),
            P(("groups", "dp")),
            P(),
            P(),
            P(("groups", "dp"), None),
        ),
        out_specs=(P(("groups", "dp"), None), P(("groups", "dp"), None)),
        check_vma=False,
    )
```

```python
import functools

import jax
import jax.numpy as jnp
from jax import lax
from jax.experimental import pallas as pl
from jax.experimental.pallas import tpu as pltpu
from jax.sharding import PartitionSpec as P

LANES = 128
HALVES = 2
MESH = pl.DeviceIdType.MESH


def chunk_count(width):
    for count in (7, 4, 2, 1):
        if width % (count * LANES) == 0:
            return count
    return 1


def dot_last(a, b):
    return lax.dot_general(a, b, (((1,), (1,)), ((), ())), preferred_element_type=jnp.float32)


def dot_first(a, b):
    return lax.dot_general(a, b, (((0,), (0,)), ((), ())), preferred_element_type=jnp.float32)


def hi_lo(a):
    hi = a.astype(jnp.bfloat16)
    return hi, (a - hi.astype(jnp.float32)).astype(jnp.bfloat16)


def kernel(
    n, k_in, k_out,
    len_ref, x_hbm, g_hbm, pin_hbm, pout_hbm, test_hbm,
    blocks, scale_ref, scores_ref,
    x_v, g_v, pin_v, pout_v, test_v,
    gath0, gath1, gtest,
    wide, wide_test, test_rows, fold, own, own_test,
    sem_x, sem_g, sem_pin, sem_pout, sem_test,
    send, recv,
):
    seqs, seq_len, _ = x_hbm.shape
    per = seqs // HALVES
    group_rows = LANES // k_in
    features = k_in * k_out
    nb = features // LANES
    chunks = g_v.shape[1]
    width = g_v.shape[4]
    all_seqs = n * seqs

    me = lax.axis_index("dp")
    groups_me = lax.axis_index("groups")
    def peer(k):
        return lax.rem(me + k, n)

    def x_copy(h):
        return pltpu.make_async_copy(x_hbm.at[pl.ds(h * per, per)], x_v.at[h], sem_x.at[h])

    def g_copy(h, c):
        start = pl.multiple_of(c * width, LANES)
        return pltpu.make_async_copy(
            g_hbm.at[pl.ds(h * per, per), :, pl.ds(start, width)], g_v.at[h, c], sem_g.at[h, c]
        )

    def pout_copy(c):
        start = pl.multiple_of(c * width, LANES)
        return pltpu.make_async_copy(pout_hbm.at[:, pl.ds(start, width)], pout_v.at[c], sem_pout.at[c])

    pin_copy = pltpu.make_async_copy(pin_hbm, pin_v, sem_pin)

    test_copy = pltpu.make_async_copy(test_hbm, test_v, sem_test)

    barrier = pltpu.get_barrier_semaphore()

    @pl.loop(1, n)
    def _(k):
        pl.semaphore_signal(barrier, inc=1, device_id=(groups_me, peer(k)), device_id_type=MESH)

    test_copy.start()
    pin_copy.start()
    x_copy(0).start()

    @pl.loop(0, chunks)
    def _(c):
        pout_copy(c).start()
        g_copy(0, c).start()

    x_copy(1).start()

    @pl.loop(0, chunks)
    def _(c):
        g_copy(1, c).start()

    test_copy.wait()
    test_wide = test_v[...].astype(jnp.float32)
    for b in range(nb):
        own_test[pl.ds(b, seqs, stride=nb), :] = test_wide[:, b * LANES:(b + 1) * LANES]
    gtest[me] = own_test[...].astype(jnp.bfloat16)

    pl.semaphore_wait(barrier, n - 1)

    def push(kind, buf, k):
        return pltpu.make_async_remote_copy(
            src_ref=buf.at[me], dst_ref=buf.at[me],
            send_sem=send.at[kind, k], recv_sem=recv.at[kind, me],
            device_id=(groups_me, peer(k)), device_id_type=MESH,
        )

    def pull(kind, buf, k):
        src = peer(k)
        return pltpu.make_async_remote_copy(
            src_ref=buf.at[src], dst_ref=buf.at[src],
            send_sem=send.at[kind, k], recv_sem=recv.at[kind, src],
            device_id=(groups_me, src), device_id_type=MESH,
        )

    def send_own(kind, buf):
        @pl.loop(1, n)
        def _(k):
            push(kind, buf, k).start()

    def rest(kind, buf):
        @pl.loop(1, n)
        def _(k):
            pull(kind, buf, k).wait_recv()

    def drain(kind, buf):
        @pl.loop(1, n)
        def _(k):
            push(kind, buf, k).wait_send()

    send_own(0, gtest)

    lane = lax.broadcasted_iota(jnp.int32, (nb, LANES), 1) // k_in
    token = lax.broadcasted_iota(jnp.int32, (seq_len, k_out), 0)

    pin_copy.wait()

    def right_part(h, low, high, total, first):
        def step(c, total):
            if first:
                pout_copy(c).wait()
            g_copy(h, c).wait()
            return total + dot_last(g_v[h, c].reshape(per * seq_len, width), pout_v[c])
        return lax.fori_loop(low, high, step, total)

    def finish(h, left, right, buf):
        for q in range(per):
            s = h * per + q
            rows = slice(q * seq_len, (q + 1) * seq_len)
            live = jnp.where(token < len_ref[s], right[rows], 0.0)
            rh, rl = hi_lo(live)
            lh, ll = hi_lo(left[rows])
            prod = dot_first(
                jnp.concatenate([rh, rh, rl], axis=0), jnp.concatenate([lh, ll, lh], axis=0)
            )
            fold[q] = prod
            tile = fold[q, pl.ds(0, nb, stride=group_rows), :]
            for k in range(1, group_rows):
                tile = jnp.where(lane == k, fold[q, pl.ds(k, nb, stride=group_rows), :], tile)
            tile = tile.astype(jnp.bfloat16)
            buf[me, q * nb:(q + 1) * nb, :] = tile
            own[s * nb:(s + 1) * nb, :] = tile.astype(jnp.float32)

    def left_part(h):
        x_copy(h).wait()
        pin = jnp.concatenate([pin_v[...]] * group_rows, axis=0)
        return dot_last(x_v[h].reshape(per * seq_len, x_v.shape[3]), pin)

    zero = jnp.zeros((per * seq_len, k_out), jnp.float32)
    mid = (chunks + 1) // 2

    left = left_part(0)
    right = right_part(0, 0, chunks, zero, True)
    finish(0, left, right, gath0)
    send_own(1, gath0)

    left = left_part(1)
    right = right_part(1, 0, mid, zero, False)
    right = right_part(1, mid, chunks, right, False)
    finish(1, left, right, gath1)
    send_own(2, gath1)

    rest(0, gtest)
    wide_test[...] = gtest[...].reshape(wide_test.shape).astype(jnp.float32)
    squares = jnp.zeros((all_seqs, LANES), jnp.float32)
    for b in range(nb):
        rows = wide_test[pl.ds(b, all_seqs, stride=nb), :]
        squares += rows * rows
        test_rows[:, b * LANES:(b + 1) * LANES] = rows.astype(jnp.bfloat16)
    own_rows = [own[pl.ds(b, seqs, stride=nb), :] for b in range(nb)]
    own_squares = own_rows[0] * own_rows[0]
    for b in range(1, nb):
        own_squares += own_rows[b] * own_rows[b]
    mean_train = jnp.sum(own_squares, axis=1, keepdims=True) / features
    mean_test = lax.dot_general(
        jnp.ones((seqs, LANES), jnp.float32), squares, (((1,), (1,)), ((), ())),
        precision=lax.Precision.HIGHEST, preferred_element_type=jnp.float32,
    ) / features
    inner = dot_last(jnp.concatenate(own_rows, axis=1).astype(jnp.bfloat16), test_rows[...])
    scores_ref[...] = inner / (
        jnp.sqrt(mean_train + 1e-06) * jnp.sqrt(mean_test + 1e-06) * jnp.sqrt(jnp.float32(features))
    )

    rest(1, gath0)
    half_rows = n * per * nb
    half_seqs = n * per

    def spread(h, buf):
        wide[pl.ds(h * half_rows, half_rows), :] = buf[...].reshape(half_rows, LANES).astype(jnp.float32)
        total = jnp.zeros((half_seqs, LANES), jnp.float32)
        for b in range(nb):
            rows = wide[pl.ds(h * half_rows + b, half_seqs, stride=nb), :]
            total += rows * rows
            blocks[b, h * half_seqs:(h + 1) * half_seqs, :] = rows.astype(jnp.bfloat16)
        return total

    total = spread(0, gath0)
    rest(2, gath1)
    total += spread(1, gath1)
    scale = features / jnp.sum(total)

    scale_ref[...] = jnp.full(scale_ref.shape, scale, jnp.float32)

    drain(0, gtest)
    drain(1, gath0)
    drain(2, gath1)


def gram_kernel(blocks, scale_ref, scores_in, fisher_ref, scores_ref, gram_tmp):
    me = lax.axis_index("dp")
    nb = blocks.shape[0]
    scale = scale_ref[0:1, :]
    scores_ref[...] = scores_in[...]
    row_count = fisher_ref.shape[0]
    first_row = me * row_count
    if row_count % LANES == 0:
        for r in range(row_count // LANES):
            mine = blocks[first_row // LANES + r]
            for b in range(nb):
                fisher_ref[r * LANES:(r + 1) * LANES, b * LANES:(b + 1) * LANES] = (
                    dot_first(mine, blocks[b]) * scale
                )
    else:
        mine = blocks[first_row // LANES]
        offset = pl.multiple_of(lax.rem(first_row, LANES), row_count)
        for b in range(nb):
            gram_tmp[...] = dot_first(mine, blocks[b]) * scale
            fisher_ref[:, b * LANES:(b + 1) * LANES] = gram_tmp[pl.ds(offset, row_count), :]


def local(layer_inputs, out_grads, lengths, p_in, p_out, test_proj):
    n = lax.axis_size("dp")
    seqs, seq_len, model_width = layer_inputs.shape
    hidden = out_grads.shape[2]
    k_in, k_out = p_in.shape[0], p_out.shape[0]
    features = k_in * k_out
    nb = features // LANES
    chunks = chunk_count(hidden)
    width = hidden // chunks
    per = seqs // HALVES
    f32, bf16 = jnp.float32, jnp.bfloat16
    dma = pltpu.SemaphoreType.DMA
    anywhere = pl.BlockSpec(memory_space=pltpu.HBM)
    vmem = pl.BlockSpec(memory_space=pltpu.VMEM)
    blocks, scale, scores = pl.pallas_call(
        functools.partial(kernel, n, k_in, k_out),
        out_shape=(
            jax.ShapeDtypeStruct((nb, n * seqs, LANES), bf16),
            jax.ShapeDtypeStruct((8, LANES), f32),
            jax.ShapeDtypeStruct((seqs, n * seqs), f32),
        ),
        in_specs=[pl.BlockSpec(memory_space=pltpu.SMEM)] + [anywhere] * 5,
        out_specs=(vmem, vmem, vmem),
        scratch_shapes=[
            pltpu.VMEM((HALVES, per, seq_len, model_width), bf16),
            pltpu.VMEM((HALVES, chunks, per, seq_len, width), bf16),
            pltpu.VMEM((k_in, model_width), bf16),
            pltpu.VMEM((chunks, k_out, width), bf16),
            pltpu.VMEM((seqs, features), bf16),
            pltpu.VMEM((n, per * nb, LANES), bf16),
            pltpu.VMEM((n, per * nb, LANES), bf16),
            pltpu.VMEM((n, seqs * nb, LANES), bf16),
            pltpu.VMEM((n * seqs * nb, LANES), f32),
            pltpu.VMEM((n * seqs * nb, LANES), f32),
            pltpu.VMEM((n * seqs, features), bf16),
            pltpu.VMEM((per, k_out, LANES), f32),
            pltpu.VMEM((seqs * nb, LANES), f32),
            pltpu.VMEM((seqs * nb, LANES), f32),
            dma((HALVES,)),
            dma((HALVES, chunks)),
            dma,
            dma((chunks,)),
            dma,
            dma((3, n)),
            dma((3, n)),
        ],
        compiler_params=pltpu.CompilerParams(
            collective_id=0, has_side_effects=True, vmem_limit_bytes=57 * 1024 * 1024
        ),
        cost_estimate=pl.CostEstimate(
            flops=2 * seqs * seq_len * (hidden * k_out + model_width * k_in),
            bytes_accessed=2 * (seqs * seq_len + k_out) * hidden,
            transcendentals=0,
        ),
    )(lengths, layer_inputs, out_grads, p_in, p_out, test_proj)
    return pl.pallas_call(
        gram_kernel,
        out_shape=(
            jax.ShapeDtypeStruct((features // n, features), f32),
            jax.ShapeDtypeStruct(scores.shape, f32),
        ),
        in_specs=[vmem, vmem, vmem],
        out_specs=(vmem, vmem),
        scratch_shapes=[pltpu.VMEM((LANES, LANES), f32)],
        compiler_params=pltpu.CompilerParams(vmem_limit_bytes=57 * 1024 * 1024),
    )(blocks, scale, scores)


def solution(mesh):
    return jax.shard_map(
        local,
        mesh=mesh,
        in_specs=(
            P(("groups", "dp"), None, None),
            P(("groups", "dp"), None, None),
            P(("groups", "dp")),
            P(),
            P(),
            P(("groups", "dp"), None),
        ),
        out_specs=(P(("groups", "dp"), None), P(("groups", "dp"), None)),
        check_vma=False,
    )
```
